32 devices in a mesh: nodes: 8 (over z, x), feat: 4 (over y, core).
Axes of the slice: x: 2, y: 2, z: 4, core: 2. Of those that a mesh axis runs over, the one named last changes fastest.
Arguments:
- features: bfloat16 [7680, 8, 602], P('nodes', 'feat'), may hold values from -6 to 6
- adjacency: int32 [7680, 8, 7680], P('nodes', 'feat'), may hold values from 0 to 2, as said below
- alpha_hits: int32 [7680, 8], P('nodes', 'feat'), may hold values from 1 to 5
- lambda_hits: int32 [7680, 8], P('nodes', 'feat'), may hold values from 1 to 5
- train_mask: int32 [7680, 8], P('nodes', 'feat'), may hold values from 0 to 1, as said below
- labels: int32 [7680, 8], P('nodes', 'feat'), may hold values from 0 to 40
- w_in: float32 [602, 512], P(None, 'feat'), may hold values from -0.25 to 0.25
- w_pair: float32 [3, 512, 1024], P(None, None, 'feat'), may hold values from -0.25 to 0.25
- w_proj: float32 [3, 1024, 512], P(None, None, 'feat'), may hold values from -0.1875 to 0.1875
- w_head: float32 [512, 41], P('feat'), may hold values from -0.5 to 0.5
- m_in: float32 [602, 512], P(None, 'feat'), may hold values from -0.00061035156 to 0.00061035156
- m_pair: float32 [3, 512, 1024], P(None, None, 'feat'), may hold values from -0.00061035156 to 0.00061035156
- m_proj: float32 [3, 1024, 512], P(None, None, 'feat'), may hold values from -0.00061035156 to 0.00061035156
- m_head: float32 [512, 41], P('feat'), may hold values from -0.0012207031 to 0.0012207031
- v_in: float32 [602, 512], P(None, 'feat'), may hold values from 1.6276042e-10 to 6.5104167e-10
- v_pair: float32 [3, 512, 1024], P(None, None, 'feat'), may hold values from 1.6276042e-10 to 6.5104167e-10
- v_proj: float32 [3, 1024, 512], P(None, None, 'feat'), may hold values from 1.6276042e-10 to 6.5104167e-10
- v_head: float32 [512, 41], P('feat'), may hold values from 6.5104167e-10 to 2.6041667e-09
Outputs:
- loss_sum: float32 [], replicated
- train_count: float32 [], replicated
- new_m_in: float32 [602, 512], P(None, 'feat')
- new_v_in: float32 [602, 512], P(None, 'feat')
- new_w_in: float32 [602, 512], P(None, 'feat')
- new_m_pair: float32 [3, 512, 1024], P(None, None, 'feat')
- new_v_pair: float32 [3, 512, 1024], P(None, None, 'feat')
- new_w_pair: float32 [3, 512, 1024], P(None, None, 'feat')
- new_m_proj: float32 [3, 1024, 512], P(None, None, 'feat')
- new_v_proj: float32 [3, 1024, 512], P(None, None, 'feat')
- new_w_proj: float32 [3, 1024, 512], P(None, None, 'feat')
- new_m_head: float32 [512, 41], P('feat')
- new_v_head: float32 [512, 41], P('feat')
- new_w_head: float32 [512, 41], P('feat')
The draws below stay inside these ranges and needn't reach their ends.
Inputs may be any that keep to these rules, and one draw needn't show every extreme that they name: `adjacency`: entries are 0, 1 or 2. In each subgraph trailing nodes may be padding: their rows and columns are zero. `train_mask`: padding nodes (those with no edges at the end of a subgraph) are never training nodes.
All inputs are finite; a program needn't handle non-finite values.
Results may differ from the reference program's by a relative error of at most 0.019.
Values may be sent and summed in bfloat16 or wider, within the bound.
A program may use at most 320 MiB of HBM per device.

```python
import math
import jax
import jax.numpy as jnp
from jax import lax

D = 512
FI = 602
CLS = 41
L = 3
NB = 7680
STEP = 5
SUBS = 8


def node_limits(key):
    return jax.random.randint(jax.random.fold_in(key, 500), (SUBS,), 3 * NB // 4, NB + 1)


def draw_adjacency(key, part):
    limits = node_limits(key)
    key = jax.random.fold_in(key, 1)
    reach = min(192, NB)
    ticket = jax.random.randint(key, (NB, SUBS, NB), 0, 4 * NB)
    counts = (ticket < reach).astype(jnp.int32) + (ticket < reach // 3).astype(jnp.int32)
    target = jnp.arange(NB, dtype=jnp.int32)
    inside = (target[:, None, None] < limits[None, :, None]) & (target[None, None, :] < limits[None, :, None])
    return jnp.where(inside, counts, 0)


def draw_train_mask(key, part):
    limits = node_limits(key)
    key = jax.random.fold_in(key, 2)
    ticket = jax.random.randint(key, (NB, SUBS), 0, 1000)
    rows = jnp.arange(NB, dtype=jnp.int32)[:, None]
    graphs = jnp.arange(SUBS, dtype=jnp.int32)[None, :]
    level = (150 + 300 * rows // NB) * (SUBS + graphs) // SUBS
    return ((ticket < level) & (rows < limits[None, :])).astype(jnp.int32)


def set_ends(values, rng, smallest, largest):
    index_at = [jax.random.randint(jax.random.fold_in(rng, axis), (), 0, length) for axis, length in enumerate(values.shape)]
    widest = values.shape.index(max(values.shape))
    neighbour = index_at[:widest] + [(index_at[widest] + 1) % values.shape[widest]] + index_at[widest + 1:]
    return values.at[tuple(index_at)].set(smallest).at[tuple(neighbour)].set(largest)


def block_levels(key, shape, pieces, low, high):
    loudness = 1.0
    for position, blocks in pieces:
        steps = jax.random.uniform(jax.random.fold_in(jax.random.fold_in(key, 6), position), (blocks,), jnp.float32, low / len(pieces), high / len(pieces))
        loudness = loudness * jnp.repeat(jnp.exp(steps), shape[position] // blocks).reshape((-1,) + (1,) * (len(shape) - 1 - position))
    return loudness


def centred(stream_key, dims, spread, most, split=(), kind=jnp.bfloat16):
    values = jax.random.normal(stream_key, dims, jnp.float32) * spread
    if len(split) > 0:
        values = block_levels(stream_key, dims, split, -0.22, 0.18) * values
    return jnp.clip(values, min=-most, max=most).astype(kind)


def setup_inputs(seed: int = 0) -> dict:
    splits = jax.random.split(jax.random.key(seed), 19)
    features = centred(splits[0], (NB, SUBS, FI), 1.0, 6.0, ((0, 8), (1, 4)))
    adjacency = draw_adjacency(jax.random.fold_in(splits[18], 71), 0)
    alpha_hits = set_ends(jax.random.randint(splits[2], (NB, SUBS), 1, 6), jax.random.fold_in(splits[2], 1), 1, 5).astype(jnp.int32)
    lambda_hits = set_ends(jax.random.randint(splits[3], (NB, SUBS), 1, 6), jax.random.fold_in(splits[3], 1), 1, 5).astype(jnp.int32)
    train_mask = draw_train_mask(jax.random.fold_in(splits[18], 71), 0)
    labels = set_ends(jax.random.randint(splits[5], (NB, SUBS), 0, CLS), jax.random.fold_in(splits[5], 1), 0, CLS - 1).astype(jnp.int32)
    w_in = centred(splits[6], (FI, D), FI ** -0.5, 0.25, ((1, 4),), jnp.float32)
    w_pair = centred(splits[7], (L, D, 2 * D), D ** -0.5, 0.25, ((2, 4),), jnp.float32)
    w_proj = centred(splits[8], (L, 2 * D, D), (2 * D) ** -0.5, 0.1875, ((2, 4),), jnp.float32)
    w_head = centred(splits[9], (D, CLS), (D // 4) ** -0.5, 0.5, ((0, 4),), jnp.float32)
    m_in = centred(splits[10], (FI, D), (0.01 / (NB * SUBS) ** 0.5), 0.00061035156, ((1, 4),), jnp.float32)
    m_pair = centred(splits[11], (L, D, 2 * D), (0.01 / (NB * SUBS) ** 0.5), 0.00061035156, ((2, 4),), jnp.float32)
    m_proj = centred(splits[12], (L, 2 * D, D), (0.01 / (NB * SUBS) ** 0.5), 0.00061035156, ((2, 4),), jnp.float32)
    m_head = centred(splits[13], (D, CLS), (0.02 / (NB * SUBS) ** 0.5), 0.0012207031, ((0, 4),), jnp.float32)
    v_in = jnp.clip(jnp.exp(math.log(6.510416650229445e-10) - 1.3862944 * jax.random.uniform(splits[14], (FI, D), jnp.float32) ** block_levels(splits[14], (FI, D), ((1, 4),), -0.2, 0.2)), 1.6276041625573612e-10, 6.510416650229445e-10)
    v_pair = jnp.clip(jnp.exp(math.log(6.510416650229445e-10) - 1.3862944 * jax.random.uniform(splits[15], (L, D, 2 * D), jnp.float32) ** block_levels(splits[15], (L, D, 2 * D), ((2, 4),), -0.2, 0.2)), 1.6276041625573612e-10, 6.510416650229445e-10)
    v_proj = jnp.clip(jnp.exp(math.log(6.510416650229445e-10) - 1.3862944 * jax.random.uniform(splits[16], (L, 2 * D, D), jnp.float32) ** block_levels(splits[16], (L, 2 * D, D), ((2, 4),), -0.2, 0.2)), 1.6276041625573612e-10, 6.510416650229445e-10)
    v_head = jnp.clip(jnp.exp(math.log(2.604166660091778e-09) - 1.3862944 * jax.random.uniform(splits[17], (D, CLS), jnp.float32) ** block_levels(splits[17], (D, CLS), ((0, 4),), -0.2, 0.2)), 6.510416650229445e-10, 2.604166660091778e-09)
    return dict(features=features, adjacency=adjacency, alpha_hits=alpha_hits, lambda_hits=lambda_hits, train_mask=train_mask, labels=labels, w_in=w_in, w_pair=w_pair, w_proj=w_proj, w_head=w_head, m_in=m_in, m_pair=m_pair, m_proj=m_proj, m_head=m_head, v_in=v_in, v_pair=v_pair, v_proj=v_proj, v_head=v_head)


B1 = 0.9
B2 = 0.999
ADAM_EPS = 1e-06
DECAY = 0.01
RATE = 0.5
SMOOTH = 0.1
NORM_EPS = 1e-06

@jax.custom_vjp
def low(v):
    return lax.optimization_barrier(v.astype(jnp.bfloat16)).astype(jnp.float32)

@jax.custom_vjp
def low_back(v):
    return v

def low_keep(v):
    return (low(v), None)

def low_pass(kept, grad):
    return (grad,)

def back_keep(v):
    return (v, None)

def back_low(kept, grad):
    return (low(grad),)
low.defvjp(low_keep, low_pass)
low_back.defvjp(back_keep, back_low)

def mult(left, right):
    return jnp.dot(left, right, precision=lax.Precision.HIGHEST)

def activate(z):
    act = jax.nn.silu(z)
    return act * lax.rsqrt(lax.optimization_barrier(jnp.mean(act * act, axis=-1, keepdims=True)) + NORM_EPS)

def graph_loss(weights, feats, adj, alpha, lam, mask, lab):
    w_in, w_pair, w_proj, w_head = weights
    links = adj.astype(jnp.float32)
    inv_deg = 1.0 / jnp.maximum(lax.optimization_barrier(jnp.sum(links, axis=1)), 1.0)
    alpha_f = alpha.astype(jnp.float32)[:, None]
    hidden = low_back(mult(feats.astype(jnp.float32), low(w_in)))
    for layer in range(L):
        paired = low_back(mult(low(hidden), low(w_pair[layer])))
        message = low(paired[:, D:] / alpha_f)
        gathered = low_back(mult(links, message))
        joined = low(jnp.concatenate([paired[:, :D], gathered * inv_deg[:, None]], axis=1))
        hidden = activate(low_back(mult(joined, low(w_proj[layer]))))
    logits = low_back(mult(low(hidden), low(w_head)))
    logp = jax.nn.log_softmax(logits, axis=-1)
    onehot = (lab[:, None] == jnp.arange(CLS, dtype=jnp.int32)[None, :]).astype(jnp.float32)
    target = (1.0 - SMOOTH) * onehot + SMOOTH / CLS
    weight = mask.astype(jnp.float32) / lam.astype(jnp.float32)
    return jnp.sum(weight * -lax.optimization_barrier(jnp.sum(target * logp, axis=-1)))

def lamb(weight, grad, first, second, axes):
    first_new = B1 * first + (1.0 - B1) * grad
    second_new = B2 * second + (1.0 - B2) * grad * grad
    update = first_new / (1.0 - B1 ** STEP) / (jnp.sqrt(second_new / (1.0 - B2 ** STEP)) + ADAM_EPS) + DECAY * weight
    trust = jnp.sqrt(lax.optimization_barrier(jnp.sum(weight * weight, axis=axes, keepdims=True))) / jnp.sqrt(lax.optimization_barrier(jnp.sum(update * update, axis=axes, keepdims=True)))
    return (first_new, second_new, weight - RATE * trust * update)

def reference(features, adjacency, alpha_hits, lambda_hits, train_mask, labels, w_in, w_pair, w_proj, w_head, m_in, m_pair, m_proj, m_head, v_in, v_pair, v_proj, v_head):
    train_count = jnp.sum(train_mask.astype(jnp.float32))
    weights = (w_in, w_pair, w_proj, w_head)

    def one_graph(carry, index):
        total, grads = carry

        def pick(array):
            return lax.dynamic_index_in_dim(array, index, 1, keepdims=False)

        def loss_of(*ws):
            return graph_loss(ws, pick(features), pick(adjacency), pick(alpha_hits), pick(lambda_hits), pick(train_mask), pick(labels))
        loss, pull = jax.vjp(loss_of, *weights)
        parts = pull(jnp.ones((), loss.dtype) / train_count)
        return ((total + loss, jax.tree.map(lambda a, b: a + b, grads, tuple(parts))), None)
    start = (jnp.zeros((), jnp.float32), tuple((jnp.zeros_like(w) for w in weights)))
    (loss_sum, grads), _ = lax.scan(one_graph, start, jnp.arange(SUBS, dtype=jnp.int32))
    new_in = lamb(w_in, grads[0], m_in, v_in, (0, 1))
    new_pair = lamb(w_pair, grads[1], m_pair, v_pair, (1, 2))
    new_proj = lamb(w_proj, grads[2], m_proj, v_proj, (1, 2))
    new_head = lamb(w_head, grads[3], m_head, v_head, (0, 1))
    return (loss_sum, train_count, new_in[0], new_in[1], new_in[2], new_pair[0], new_pair[1], new_pair[2], new_proj[0], new_proj[1], new_proj[2], new_head[0], new_head[1], new_head[2])
```

```python
import functools
import jax
import jax.numpy as jnp
from jax import lax
from jax.experimental import pallas as pl
from jax.experimental.pallas import tpu as pltpu
from jax.sharding import PartitionSpec as P

STEP = 5


B1 = 0.9
B2 = 0.999
ADAM_EPS = 1e-06
DECAY = 0.01
RATE = 0.5
SMOOTH = 0.1
NORM_EPS = 1e-06
MESH = pl.DeviceIdType.MESH
BF = jnp.bfloat16
F32 = jnp.float32

def ag_kernel(Z,C,E,LIM,own,out,cp,rup,rdn,eup,edn,rxo,rxu,rxd,sup,sdn,seu,sed,sxo,sxu,sxd):
    R,W=own.shape; CH=R//C
    n=lax.axis_index("nodes"); f=lax.axis_index("feat")
    z=n//2; x=n%2
    dn=(n-2,f); up=(n+2,f); xn=(n+1-2*x,f)
    has_dn=z>0; has_up=z<Z-1
    bar=pltpu.get_barrier_semaphore()
    pl.semaphore_signal(bar,inc=1,device_id=xn,device_id_type=MESH)
    @pl.when(has_dn)
    def _(): pl.semaphore_signal(bar,inc=1,device_id=dn,device_id_type=MESH)
    @pl.when(has_up)
    def _(): pl.semaphore_signal(bar,inc=1,device_id=up,device_id_type=MESH)
    local=pltpu.make_async_copy(own,out.at[pl.ds(n*R,R)],cp)
    local.start()
    pl.semaphore_wait(bar,1+jnp.where(has_dn,1,0)+jnp.where(has_up,1,0))
    def rows(b,c): return pl.ds(b*R+c*CH,CH)
    def rc(b,c,s,r,dev,src=None):
        o=out.at[rows(b,c)]
        return pltpu.make_async_remote_copy(o if src is None else src,o,s,r,device_id=dev,device_id_type=MESH)
    def own_step(c,_):
        src=own.at[pl.ds(c*CH,CH)]
        rc(n,c,sxo.at[c],rxo.at[c],xn,src).start()
        pl.when(has_dn)(lambda: rc(n,c,sdn.at[0,c],rup.at[0,c],dn,src).start())
        pl.when(has_up)(lambda: rc(n,c,sup.at[0,c],rdn.at[0,c],up,src).start())
        return 0
    lax.fori_loop(0,C,own_step,0)
    H=Z-1
    for k in range(H):
        def step(c,_):
            bu=n+2*(1+k); bd=n-2*(1+k)
            not_extra = (c>=E) if k==0 else None
            @pl.when(z+1+k<=Z-1)
            def _():
                rc(bu,c,sdn.at[k,c],rup.at[k,c],dn).wait_recv()
                if k<H-1:
                    pl.when(has_dn)(lambda: rc(bu,c,sdn.at[k+1,c],rup.at[k+1,c],dn).start())
                fx=lambda: rc(bu,c,sxu.at[k,c],rxu.at[k,c],xn).start()
                fx() if k else pl.when(c>=E)(fx)
            @pl.when(z-1-k>=0)
            def _():
                rc(bd,c,sup.at[k,c],rdn.at[k,c],up).wait_recv()
                if k<H-1:
                    pl.when(has_up)(lambda: rc(bd,c,sup.at[k+1,c],rdn.at[k+1,c],up).start())
                fx=lambda: rc(bd,c,sxd.at[k,c],rxd.at[k,c],xn).start()
                fx() if k else pl.when(c>=E)(fx)
            return 0
        lax.fori_loop(0,C,step,0)
    bx=n+1-2*x
    def ex(c,_):
        rc(bx,c,sxo.at[c],rxo.at[c],xn).wait_recv()
        pl.when(has_dn)(lambda: rc(bx,c,sed.at[c],eup.at[c],dn).start())
        pl.when(has_up)(lambda: rc(bx,c,seu.at[c],edn.at[c],up).start())
        return 0
    lax.fori_loop(0,E,ex,0)
    def drain_own(c,_):
        rc(n,c,sxo.at[c],rxo.at[c],xn).wait_send()
        pl.when(c>=E)(lambda: rc(n,c,sxo.at[c],rxo.at[c],xn).wait_recv())
        pl.when(has_dn)(lambda: rc(n,c,sdn.at[0,c],rup.at[0,c],dn).wait_send())
        pl.when(has_up)(lambda: rc(n,c,sup.at[0,c],rdn.at[0,c],up).wait_send())
        return 0
    lax.fori_loop(0,C,drain_own,0)
    for k in range(H):
        def drain(c,_):
            def w(cond,sem_s,sem_r):
                pass
            @pl.when(z+1+k<=Z-1)
            def _():
                if k<H-1: pl.when(has_dn)(lambda: rc(n,c,sdn.at[k+1,c],rup.at[0,c],dn).wait_send())
                def g():
                    d=rc(n,c,sxu.at[k,c],rxu.at[k,c],xn); d.wait_send(); d.wait_recv()
                g() if k else pl.when(c>=E)(g)
                if k==0:
                    pl.when(c<E)(lambda: rc(n,c,sed.at[c],eup.at[c],dn).wait_recv())
            @pl.when(z-1-k>=0)
            def _():
                if k<H-1: pl.when(has_up)(lambda: rc(n,c,sup.at[k+1,c],rdn.at[0,c],up).wait_send())
                def g():
                    d=rc(n,c,sxd.at[k,c],rxd.at[k,c],xn); d.wait_send(); d.wait_recv()
                g() if k else pl.when(c>=E)(g)
                if k==0:
                    pl.when(c<E)(lambda: rc(n,c,seu.at[c],edn.at[c],up).wait_recv())
            return 0
        lax.fori_loop(0,C,drain,0)
    def drain_ex(c,_):
        pl.when(has_dn)(lambda: rc(bx,c,sed.at[c],eup.at[c],dn).wait_send())
        pl.when(has_up)(lambda: rc(bx,c,seu.at[c],edn.at[c],up).wait_send())
        return 0
    lax.fori_loop(0,E,drain_ex,0)
    local.wait()
def ag(a,cid,C,E,N=8,vm=False):
    R,W=a.shape; Z=N//2
    D=pltpu.SemaphoreType.DMA
    sems=[D((Z-1,C)),D((Z-1,C)),D((C,)),D((C,)),D((C,)),D((Z-1,C)),D((Z-1,C))]
    return pl.pallas_call(functools.partial(ag_kernel,Z,C,E,0),
        out_shape=jax.ShapeDtypeStruct((N*R,W),a.dtype),
        in_specs=[pl.BlockSpec(memory_space=pltpu.VMEM)],out_specs=pl.BlockSpec(memory_space=pltpu.VMEM if vm else pl.ANY),
        scratch_shapes=[D]+sems+sems,
        compiler_params=pltpu.CompilerParams(collective_id=cid,has_side_effects=True,vmem_limit_bytes=48*2**20))(a)


def activate(z):
    act = jax.nn.silu(z)
    return act * lax.rsqrt(jnp.mean(act * act, axis=-1, keepdims=True) + NORM_EPS)


def mm(a, b):
    return jnp.dot(a, b, preferred_element_type=F32)


def mm_nt(a, b):
    return lax.dot_general(a, b, (((1,), (1,)), ((), ())), preferred_element_type=F32)


def mm_tn(a, b):
    return lax.dot_general(a, b, (((0,), (0,)), ((), ())), preferred_element_type=F32)


def lamb_parts(weight, grad, first, second):
    first_new = B1 * first + (1.0 - B1) * grad
    second_new = B2 * second + (1.0 - B2) * grad * grad
    update = (
        first_new / (1.0 - B1**STEP) / (jnp.sqrt(second_new / (1.0 - B2**STEP)) + ADAM_EPS)
        + DECAY * weight
    )
    return (first_new, second_new, update)


def update(weights, firsts, seconds, grads, layers):
    w_in, w_pair, w_proj, w_head = weights
    parts = [lamb_parts(*t) for t in zip(weights, grads, firsts, seconds)]

    def squares(four):
        return jnp.concatenate(
            [
                jnp.sum(four[0] * four[0])[None],
                jnp.sum(four[1] * four[1], axis=(1, 2)),
                jnp.sum(four[2] * four[2], axis=(1, 2)),
                jnp.sum(four[3] * four[3])[None],
            ]
        )

    norms = lax.psum(jnp.stack([squares(weights), squares([p[2] for p in parts])]), "feat")
    trust = jnp.sqrt(norms[0]) / jnp.sqrt(norms[1])
    rates = [
        trust[0],
        trust[1 : 1 + layers][:, None, None],
        trust[1 + layers : 1 + 2 * layers][:, None, None],
        trust[1 + 2 * layers],
    ]
    outs = []
    for w, p, t in zip(weights, parts, rates):
        outs += [p[0], p[1], w - RATE * t * p[2]]
    return tuple(outs)


def reduce_grads(grads, dims):
    return [
        lax.psum(
            lax.psum_scatter(g.astype(BF), "feat", scatter_dimension=d, tiled=True), "nodes"
        ).astype(F32)
        for g, d in zip(grads, dims)
    ]


def body(gather, scatter, *args):
    features, adjacency, alpha_hits, lambda_hits, train_mask, labels = args[:6]
    weights, firsts, seconds = args[6:10], args[10:14], args[14:18]
    full_in, full_pair, full_proj, full_head = (
        lax.all_gather(w.astype(BF), "feat", axis=d, tiled=True)
        for w, d in zip(weights, (1, 2, 2, 0))
    )
    layers, width = full_pair.shape[0], full_pair.shape[1]
    classes = full_head.shape[1]
    subs = features.shape[1]
    ids = range(subs)
    alpha = [alpha_hits[:, s].astype(F32)[:, None] for s in ids]
    feats = [features[:, s, :] for s in ids]
    wide = -(-feats[0].shape[1] // 128) * 128 - feats[0].shape[1]
    far = [
        gather(jnp.pad((feats[s].astype(F32) / alpha[s]).astype(BF), ((0, 0), (0, wide))), s)
        for s in ids
    ]
    links = [adjacency[:, s, :].astype(BF) for s in ids]
    inv_deg = [
        1.0 / jnp.maximum(jnp.sum(adjacency[:, s, :], axis=1).astype(F32), 1.0)[:, None]
        for s in ids
    ]
    weight = train_mask.astype(F32) / lambda_hits.astype(F32)
    train_count = lax.psum(jnp.sum(train_mask.astype(F32)), ("nodes", "feat"))
    kept = [[] for _ in ids]
    near = [mm(links[s], far[s])[:, : feats[s].shape[1]].astype(BF) for s in ids]
    hidden = [mm(feats[s], full_in).astype(BF) for s in ids]
    pulled = [mm(near[s], full_in).astype(BF) for s in ids]
    for layer in range(layers):
        top, bottom = full_proj[layer][:width], full_proj[layer][width:]
        for s in ids:
            if layer == 0:
                self_v = mm(hidden[s], full_pair[0][:, :width]).astype(BF)
                agg = mm(pulled[s], full_pair[0][:, width:])
            else:
                paired = mm(hidden[s], full_pair[layer])
                self_v = paired[:, :width].astype(BF)
                message = (paired[:, width:] / alpha[s]).astype(BF)
                agg = mm(links[s], gather(message, s))
            mean_v = (agg * inv_deg[s]).astype(BF)
            z = mm(self_v, top) + mm(mean_v, bottom)
            kept[s].append((hidden[s], self_v, mean_v, z))
            hidden[s] = activate(z).astype(BF)
    loss = 0.0
    grad_in = 0.0
    grad_head = 0.0
    grad_pair = [0.0] * layers
    grad_proj = [0.0] * layers
    grad_h = []
    for s in ids:
        logits = mm(hidden[s], full_head)
        logp = jax.nn.log_softmax(logits, axis=-1)
        onehot = (labels[:, s][:, None] == jnp.arange(classes, dtype=jnp.int32)).astype(F32)
        target = (1.0 - SMOOTH) * onehot + SMOOTH / classes
        loss = loss + jnp.sum(weight[:, s] * -jnp.sum(target * logp, axis=-1))
        grad_logits = ((weight[:, s] / train_count)[:, None] * (jnp.exp(logp) - target)).astype(BF)
        grad_head = grad_head + mm_tn(hidden[s], grad_logits)
        grad_h.append(mm_nt(grad_logits, full_head))
    for layer in reversed(range(layers)):
        top, bottom = full_proj[layer][:width], full_proj[layer][width:]
        w_self, w_far = full_pair[layer][:, :width], full_pair[layer][:, width:]
        for s in ids:
            hidden_b, self_v, mean_v, z = kept[s][layer]
            _, pull = jax.vjp(activate, z)
            grad_z = pull(grad_h[s])[0].astype(BF)
            grad_proj[layer] = grad_proj[layer] + jnp.concatenate(
                [mm_tn(self_v, grad_z), mm_tn(mean_v, grad_z)]
            )
            grad_self = mm_nt(grad_z, top).astype(BF)
            grad_agg = (mm_nt(grad_z, bottom) * inv_deg[s]).astype(BF)
            if layer == 0:
                grad_pair[0] = grad_pair[0] + jnp.concatenate(
                    [mm_tn(hidden_b, grad_self), mm_tn(pulled[s], grad_agg)], axis=1
                )
                grad_in = (
                    grad_in
                    + mm_tn(feats[s], mm_nt(grad_self, w_self).astype(BF))
                    + mm_tn(near[s], mm_nt(grad_agg, w_far).astype(BF))
                )
            else:
                grad_message = scatter(mm_tn(links[s], grad_agg).astype(BF), s).astype(F32)
                grad_far = (grad_message / alpha[s]).astype(BF)
                grad_pair[layer] = grad_pair[layer] + jnp.concatenate(
                    [mm_tn(hidden_b, grad_self), mm_tn(hidden_b, grad_far)], axis=1
                )
                grad_h[s] = mm_nt(grad_self, w_self) + mm_nt(grad_far, w_far)
    loss_sum = lax.psum(loss, ("nodes", "feat"))
    grads = reduce_grads(
        [grad_in, jnp.stack(grad_pair), jnp.stack(grad_proj), grad_head], (1, 2, 2, 0)
    )
    return (loss_sum, train_count, *update(weights, firsts, seconds, grads, layers))


def solution(mesh):
    nodes = mesh.shape["nodes"]

    def gather(x, s):
        if nodes != 8:
            return lax.all_gather(x, "nodes", axis=0, tiled=True)
        return ag(x, x.shape[1] // 128, 6, 3)

    def scatter(x, s):
        return lax.psum_scatter(x, "nodes", scatter_dimension=0, tiled=True)

    row = (P("nodes", "feat", None),) * 2 + (P("nodes", "feat"),) * 4
    by_weight = (P(None, "feat"), P(None, None, "feat"), P(None, None, "feat"), P("feat", None))
    return jax.shard_map(
        functools.partial(body, gather, scatter),
        mesh=mesh,
        in_specs=row + by_weight * 3,
        out_specs=(P(), P()) + tuple(spec for spec in by_weight for _ in range(3)),
        check_vma=False,
    )
```
